32 devices in a mesh: dp: 8 (over z, y), ctx: 4 (over x, core).
Axes of the slice: x: 2, y: 2, z: 4, core: 2. Of those that a mesh axis runs over, the one named last changes fastest.
Arguments:
- tokens: bfloat16 [8, 1024, 1024], P('dp', 'ctx'), may hold values from -6 to 6
- cotangent: bfloat16 [8, 1024, 1024], P('dp', 'ctx'), may hold values from -6 to 6
- expander: bfloat16 [3432448], P(('dp', 'ctx')), may hold values from -0.1875 to 0.1875
- convolver: bfloat16 [8960], P(('dp', 'ctx')), may hold values from -3 to 3
- contractor: bfloat16 [1572864], P(('dp', 'ctx')), may hold values from -0.15625 to 0.15625
- projector: bfloat16 [786432], P(('dp', 'ctx')), may hold values from -0.1875 to 0.1875
- combiner: bfloat16 [524288], P(('dp', 'ctx')), may hold values from -1 to 1
- widener: bfloat16 [4194304], P(('dp', 'ctx')), may hold values from -0.1875 to 0.1875
- narrower: bfloat16 [2097152], P(('dp', 'ctx')), may hold values from -0.125 to 0.125
- norm_gains: bfloat16 [3584], P(('dp', 'ctx')), may hold values from 0.5 to 1.5
- head_rates: float32 [3, 24], replicated, may hold values from -6 to 2
Outputs:
- layer_output: bfloat16 [8, 1024, 1024], P('dp', 'ctx')
- input_gradient: float32 [8, 1024, 1024], P('dp', 'ctx')
- expander_grad: float32 [3432448], P(('dp', 'ctx'))
- convolver_grad: float32 [8960], P(('dp', 'ctx'))
- contractor_grad: float32 [1572864], P(('dp', 'ctx'))
- projector_grad: float32 [786432], P(('dp', 'ctx'))
- combiner_grad: float32 [524288], P(('dp', 'ctx'))
- widener_grad: float32 [4194304], P(('dp', 'ctx'))
- narrower_grad: float32 [2097152], P(('dp', 'ctx'))
- gains_grad: float32 [3584], P(('dp', 'ctx'))
- rates_grad: float32 [3, 24], replicated
The draws below stay inside these ranges and needn't reach their ends.
All inputs are finite; a program needn't handle non-finite values.
Results may differ from the reference program's by a relative error of at most 0.014.
Values may be sent and summed in bfloat16 or wider, within the bound.
A program may use at most 256 MiB of HBM per device.

```python
import jax
import jax.numpy as jnp
from jax import lax

D = 1024
MHEADS = 24
MDIM = 64
STATE = 128
KCONV = 4
AHEADS = 8
KVHEADS = 2
ADIM = 64
FF = 2048
SPAN = 128
SEQ_LEN = 1024
DINNER = 1536
CONV_CH = 1792
PROJ = 3352
SEQS = 8


def draw_head_rates(key, part):
    key = jax.random.fold_in(key, 7)
    first_key, second_key, third_key = jax.random.split(key, 3)
    step_bias = jax.random.uniform(first_key, (MHEADS,), jnp.float32, -3.0, -1.5)
    log_rate = jax.random.uniform(second_key, (MHEADS,), jnp.float32, -5.0, -0.5)
    skip_gain = jax.random.uniform(third_key, (MHEADS,), jnp.float32, 0.5, 1.5)
    return jnp.stack([step_bias, log_rate, skip_gain], 0)


def block_levels(stream_key, dims, pieces, least, high):
    level, own = 1.0, jax.random.fold_in(stream_key, 6)
    for axis_at, blocks in pieces:
        steps = jnp.exp(jax.random.uniform(jax.random.fold_in(own, axis_at), (blocks,), jnp.float32, least / len(pieces), high / len(pieces)))
        level = level * jnp.repeat(steps, dims[axis_at] // blocks).reshape([-1 if axis == axis_at else 1 for axis in range(len(dims))])
    return level


def noise(own_key, dims, deviation, most, shards=(), dtype=jnp.bfloat16):
    values = deviation * jax.random.normal(own_key, dims, jnp.float32)
    if shards:
        values = values * block_levels(own_key, dims, shards, -0.22, 0.18)
    return jnp.clip(values, -most, most).astype(dtype)


def setup_inputs(seed: int = 0) -> dict:
    key_list = jax.random.split(jax.random.key(seed), 12)
    tokens = noise(key_list[0], (SEQS, SEQ_LEN, D), 1.0, 6.0, ((0, 8), (1, 4)))
    cotangent = noise(key_list[1], (SEQS, SEQ_LEN, D), 1.0, 6.0, ((0, 8), (1, 4)))
    expander = noise(key_list[2], (D * PROJ,), D ** -0.5, 0.1875, ((0, 32),))
    convolver = noise(key_list[3], ((KCONV + 1) * CONV_CH,), KCONV ** -0.5, 3.0, ((0, 32),))
    contractor = noise(key_list[4], (DINNER * D,), DINNER ** -0.5, 0.15625, ((0, 32),))
    projector = noise(key_list[5], (D * (AHEADS + 2 * KVHEADS) * ADIM,), D ** -0.5, 0.1875, ((0, 32),))
    combiner = noise(key_list[6], (AHEADS * ADIM * D,), (AHEADS * ADIM // 16) ** -0.5, 1.0, ((0, 32),))
    widener = noise(key_list[7], (2 * D * FF,), D ** -0.5, 0.1875, ((0, 32),))
    narrower = noise(key_list[8], (FF * D,), FF ** -0.5, 0.125, ((0, 32),))
    norm_gains = jnp.clip(1.0 + 0.1 * jax.random.normal(key_list[9], (2 * D + DINNER,), jnp.float32), 0.5, 1.5).astype(jnp.bfloat16)
    head_rates = draw_head_rates(jax.random.fold_in(key_list[11], 71), 0)
    return {"tokens": tokens, "cotangent": cotangent, "expander": expander, "convolver": convolver, "contractor": contractor, "projector": projector, "combiner": combiner, "widener": widener, "narrower": narrower, "norm_gains": norm_gains, "head_rates": head_rates}


EPSILON = 1e-05
ROPE_BASE = 10000.0

@jax.custom_vjp
def low(v):
    return lax.optimization_barrier(v.astype(jnp.bfloat16)).astype(jnp.float32)

@jax.custom_vjp
def low_back(v):
    return v

def low_keep(v):
    return (low(v), None)

def low_pass(kept, grad):
    return (grad,)

def back_keep(v):
    return (v, None)

def back_low(kept, grad):
    return (low(grad),)
low.defvjp(low_keep, low_pass)
low_back.defvjp(back_keep, back_low)

def matmul(left, right):
    return jnp.dot(left, right, precision=lax.Precision.HIGHEST, preferred_element_type=jnp.float32)

def rms_scale(values):
    return lax.rsqrt(lax.optimization_barrier(jnp.mean(values * values, -1, keepdims=True)) + EPSILON)

def rotate(values, positions):
    half = values.shape[-1] // 2
    freqs = ROPE_BASE ** (-(jnp.arange(half).astype(jnp.float32) * 2.0 / values.shape[-1]))
    angles = positions[:, None] * freqs[None, :]
    cosine = jnp.cos(angles)[:, None, :]
    sine = jnp.sin(angles)[:, None, :]
    first = values[..., :half]
    second = values[..., half:]
    return jnp.concatenate([first * cosine - second * sine, second * cosine + first * sine], -1)

def span_step(state, block):
    inputs, b_proj, c_proj, step_size, log_decay = block
    cumul = jnp.cumsum(log_decay, axis=1)
    count = cumul.shape[1]
    lower = jnp.arange(count)[:, None] >= jnp.arange(count)[None, :]
    gaps = cumul[:, :, None, :] - cumul[:, None, :, :]
    decays = jnp.exp(jnp.where(lower[None, :, :, None], gaps, -jnp.inf))
    intersection = jnp.einsum('btn,bsn->bts', c_proj, b_proj, precision=lax.Precision.HIGHEST)
    mixing = intersection[..., None] * decays * step_size[:, None, :, :]
    within = jnp.einsum('btsh,bshp->bthp', mixing, inputs, precision=lax.Precision.HIGHEST)
    carried = jnp.exp(cumul)[..., None] * jnp.einsum('btn,bhpn->bthp', c_proj, state, precision=lax.Precision.HIGHEST)
    tail = jnp.exp(cumul[:, -1:, :] - cumul) * step_size
    new_state = jnp.exp(cumul[:, -1, :])[:, :, None, None] * state + jnp.einsum('bsh,bsn,bshp->bhpn', tail, b_proj, inputs, precision=lax.Precision.HIGHEST)
    return (new_state, within + carried)

def run_spans(inputs, b_proj, c_proj, step_size, log_decay, state):
    batch, length = (inputs.shape[0], inputs.shape[1])
    count = length // SPAN

    def split(values):
        return jnp.moveaxis(values.reshape((batch, count, SPAN) + values.shape[2:]), 1, 0)
    final, outputs = lax.scan(jax.checkpoint(span_step), state, (split(inputs), split(b_proj), split(c_proj), split(step_size), split(log_decay)))
    outputs = jnp.moveaxis(outputs, 0, 1).reshape(batch, length, MHEADS, MDIM)
    return (outputs, final)

def prepare(extended, conv_full, raw_step, head_rates):
    length = extended.shape[1] - (KCONV - 1)
    mixed = conv_full[KCONV]
    for offset in range(KCONV):
        mixed = mixed + conv_full[offset] * extended[:, offset:offset + length]
    activated = jax.nn.silu(mixed)
    inputs = activated[..., :DINNER].reshape(activated.shape[0], length, MHEADS, MDIM)
    b_proj = activated[..., DINNER:DINNER + STATE]
    c_proj = activated[..., DINNER + STATE:]
    step_size = jax.nn.softplus(raw_step + head_rates[0])
    log_decay = -step_size * jnp.exp(head_rates[1])
    return (inputs, b_proj, c_proj, step_size, log_decay)

def mixer(extended, conv_full, raw_step, head_rates, state):
    inputs, b_proj, c_proj, step_size, log_decay = prepare(extended, conv_full, raw_step, head_rates)
    outputs, final = run_spans(inputs, b_proj, c_proj, step_size, log_decay, state)
    return (outputs + head_rates[2][:, None] * inputs, final)

def forward(weights, stream):
    w_expand, w_conv, w_contract, w_project, w_combine, w_widen, w_narrow, gain_all, head_rates = weights
    length = stream.shape[0]
    first_gain = gain_all[:D]
    second_gain = gain_all[D:2 * D]
    mixer_gain = gain_all[2 * D:]
    normed = low(stream * rms_scale(stream) * first_gain)
    expanded = low_back(matmul(normed, w_expand))
    gate_branch = expanded[:, :DINNER]
    conv_input = low(expanded[:, DINNER:DINNER + CONV_CH])
    raw_step = expanded[:, DINNER + CONV_CH:]
    extended = jnp.concatenate([jnp.zeros((KCONV - 1, CONV_CH), jnp.float32), conv_input], 0)
    start_state = jnp.zeros((1, MHEADS, MDIM, STATE), jnp.float32)
    scanned, final = mixer(extended[None], w_conv, raw_step[None], head_rates, start_state)
    scanned = scanned[0].reshape(length, DINNER)
    gated = scanned * jax.nn.silu(gate_branch)
    gated_norm = low(gated * rms_scale(gated) * mixer_gain)
    mixer_branch = low_back(matmul(gated_norm, w_contract))
    projected = low_back(matmul(normed, w_project))
    queries = projected[:, :AHEADS * ADIM].reshape(length, AHEADS, ADIM)
    keys = projected[:, AHEADS * ADIM:(AHEADS + KVHEADS) * ADIM].reshape(length, KVHEADS, ADIM)
    values = projected[:, (AHEADS + KVHEADS) * ADIM:].reshape(length, KVHEADS, ADIM)
    positions = jnp.arange(length).astype(jnp.float32)
    queries = low(rotate(queries, positions))
    keys = low(rotate(keys, positions))
    values = low(values)
    grouped = queries.reshape(length, KVHEADS, AHEADS // KVHEADS, ADIM)
    scores = low_back(jnp.einsum('tkgd,skd->kgts', grouped, keys, precision=lax.Precision.HIGHEST) * ADIM ** (-0.5))
    causal = jnp.arange(length)[None, :] <= jnp.arange(length)[:, None]
    scores = jnp.where(causal, scores, -jnp.inf)
    probs = low(jax.nn.softmax(scores, axis=-1))
    attended = jnp.einsum('kgts,skd->tkgd', probs, values, precision=lax.Precision.HIGHEST)
    attended = low(low_back(attended.reshape(length, AHEADS * ADIM)))
    attention_branch = low_back(matmul(attended, w_combine))
    middle = stream + mixer_branch + attention_branch
    second = low(middle * rms_scale(middle) * second_gain)
    widened = low_back(matmul(second, w_widen))
    activated = low(jax.nn.silu(widened[:, :FF]) * widened[:, FF:])
    return middle + low_back(matmul(activated, w_narrow))

def reference(tokens, cotangent, expander, convolver, contractor, projector, combiner, widener, narrower, norm_gains, head_rates):
    weights = (expander.astype(jnp.float32).reshape(D, PROJ), convolver.astype(jnp.float32).reshape(KCONV + 1, CONV_CH), contractor.astype(jnp.float32).reshape(DINNER, D), projector.astype(jnp.float32).reshape(D, (AHEADS + 2 * KVHEADS) * ADIM), combiner.astype(jnp.float32).reshape(AHEADS * ADIM, D), widener.astype(jnp.float32).reshape(D, 2 * FF), narrower.astype(jnp.float32).reshape(FF, D), norm_gains.astype(jnp.float32), head_rates.astype(jnp.float32))
    zeros = jax.tree.map(jnp.zeros_like, weights)

    def per_sequence(totals, pair):
        seq_in, seq_cot = pair
        output, pullback = jax.vjp(forward, weights, seq_in.astype(jnp.float32))
        weight_grads, input_grad = pullback(seq_cot.astype(jnp.float32))
        totals = jax.tree.map(lambda left, right: left + right, totals, weight_grads)
        return (totals, (output.astype(jnp.bfloat16), input_grad))
    totals, (outputs, input_grads) = lax.scan(per_sequence, zeros, (tokens, cotangent))
    return (outputs, input_grads, totals[0].reshape(-1), totals[1].reshape(-1), totals[2].reshape(-1), totals[3].reshape(-1), totals[4].reshape(-1), totals[5].reshape(-1), totals[6].reshape(-1), totals[7], totals[8])
```

```python
import jax
import jax.numpy as jnp
from jax import lax
from jax.sharding import PartitionSpec as P

D = 1024
MHEADS = 24
MDIM = 64
STATE = 128
KCONV = 4
AHEADS = 8
KVHEADS = 2
ADIM = 64
FF = 2048
SPAN = 128
DINNER = 1536
CONV_CH = 1792
PROJ = 3352


EPSILON = 1e-05
ROPE_BASE = 10000.0


def passed_along(value, axis, steps):
    count = lax.axis_size(axis)
    leading, last = (max(0, -steps), min(count, count - steps))
    return lax.ppermute(value, axis, [(source, source + steps) for source in range(leading, last)])


def rms_scale(values):
    return lax.rsqrt(jnp.mean(values * values, -1, keepdims=True) + EPSILON)


def rms_back(values, scale, gain, grad):
    scaled = grad * gain
    values_grad = scale * scaled - values * scale**3 * jnp.mean(scaled * values, -1, keepdims=True)
    gain_grad = jnp.sum(grad * values * scale, axis=(0, 1))
    return (values_grad, gain_grad)


def rotate(values, positions):
    half = values.shape[-1] // 2
    freqs = ROPE_BASE ** (-(jnp.arange(half).astype(jnp.float32) * 2.0 / values.shape[-1]))
    angles = positions[:, None] * freqs[None, :]
    cosine = jnp.cos(angles)[:, None, :]
    sine = jnp.sin(angles)[:, None, :]
    first = values[..., :half]
    second = values[..., half:]
    return jnp.concatenate([first * cosine - second * sine, second * cosine + first * sine], -1)


def masked_scores(grouped, key_all, causal):
    raw_scores = jnp.einsum(
        "btkgd,bskd->bkgts", grouped, key_all, preferred_element_type=jnp.float32
    ) * ADIM ** (-0.5)
    return jnp.where(causal, raw_scores, -jnp.inf)


def project(left, right):
    return jnp.einsum("btd,df->btf", left, right, preferred_element_type=jnp.float32)


def project_back(left, right):
    return jnp.einsum("btf,df->btd", left, right, preferred_element_type=jnp.float32)


def outer_sum(left, right):
    return jnp.einsum("btd,btf->df", left, right, preferred_element_type=jnp.float32)


WIDE = 4224
STEP_AT = DINNER + CONV_CH + (AHEADS + 2 * KVHEADS) * ADIM
PROJ_AT = DINNER + CONV_CH
ALL = ("dp", "ctx")
HIGH = lax.Precision.HIGHEST


def gathered(shard):
    return lax.all_gather(shard, ALL, axis=0, tiled=True)


def scattered(value):
    return lax.psum_scatter(value, ALL, scatter_dimension=0, tiled=True)


def per_head(values):
    return jnp.transpose(values.reshape(values.shape[0], MHEADS, MDIM), (1, 0, 2))


def flat_heads(values):
    return jnp.transpose(values, (1, 0, 2)).reshape(values.shape[1], DINNER)


def spread(per_step):
    return jnp.repeat(per_step, MDIM, axis=1)


def headed(left, right):
    return lax.dot_general(
        left.astype(jnp.bfloat16),
        right.astype(jnp.bfloat16),
        (((2,), (1,)), ((0,), (0,))),
        preferred_element_type=jnp.float32,
    )


def headed_t(left, right):
    return lax.dot_general(
        left.astype(jnp.bfloat16),
        right.astype(jnp.bfloat16),
        (((1,), (1,)), ((0,), (0,))),
        preferred_element_type=jnp.float32,
    )


def times(left, right, dims):
    return lax.dot_general(
        left.astype(jnp.bfloat16),
        right.astype(jnp.bfloat16),
        (dims, ((), ())),
        preferred_element_type=jnp.float32,
    )


def pack_state(state, total):
    lead = total.astype(jnp.bfloat16)
    rest = (total - lead.astype(jnp.float32)).astype(jnp.bfloat16)
    extra = jnp.zeros((16, STATE), jnp.bfloat16)
    extra = extra.at[0, :MHEADS].set(lead).at[1, :MHEADS].set(rest)
    return jnp.concatenate([state.astype(jnp.bfloat16), extra], 0)


def totals_of(packed):
    parts = packed[:, DINNER : DINNER + 2, :MHEADS].astype(jnp.float32)
    return parts[:, 0] + parts[:, 1]


def head_sum(values):
    return jnp.sum(values.reshape(values.shape[0], MHEADS, MDIM), -1)


def local(
    tokens,
    cotangent,
    expander,
    convolver,
    contractor,
    projector,
    combiner,
    widener,
    narrower,
    norm_gains,
    head_rates,
):
    devices = lax.axis_size("dp") * lax.axis_size("ctx")
    ctx_count = lax.axis_size("ctx")
    here = lax.axis_index("ctx")
    batch, rows = (tokens.shape[0], tokens.shape[1])
    count = D // devices
    small = convolver.shape[0] + norm_gains.shape[0]
    small_cols = -(-small // count)
    small_at = STEP_AT + MHEADS
    small_all = jnp.pad(
        jnp.concatenate([convolver, norm_gains], 0), (0, small_cols * count - small)
    ).reshape(count, small_cols)
    expander_rows = expander.reshape(count, PROJ)
    shard_first = jnp.concatenate(
        [
            expander_rows[:, :PROJ_AT],
            projector.reshape(count, -1),
            expander_rows[:, PROJ_AT:],
            small_all,
            jnp.zeros((count, WIDE - small_at - small_cols), jnp.bfloat16),
        ],
        1,
    )
    w_first = gathered(shard_first)
    contract_rows, combine_rows, narrow_rows = (
        DINNER // devices,
        AHEADS * ADIM // devices,
        FF // devices,
    )
    shard_second = jnp.concatenate(
        [
            contractor.reshape(contract_rows, D),
            combiner.reshape(combine_rows, D),
            narrower.reshape(narrow_rows, D),
        ],
        0,
    )
    shard_second, w_first = lax.optimization_barrier((shard_second, w_first))
    w_second = gathered(shard_second[None])
    w_contract = w_second[:, :contract_rows].reshape(DINNER, D)
    w_combine = w_second[:, contract_rows : contract_rows + combine_rows].reshape(AHEADS * ADIM, D)
    w_narrow = w_second[:, contract_rows + combine_rows :].reshape(FF, D)
    shard_widen, w_second_done = lax.optimization_barrier((widener.reshape(count, 2 * FF), w_second[0, 0, 0]))
    w_widen = gathered(shard_widen)

    small_back = w_first[:, small_at : small_at + small_cols].reshape(devices, -1)
    conv_full = small_back[:, : convolver.shape[0]].reshape(KCONV + 1, CONV_CH).astype(jnp.float32)
    gains = small_back[:, convolver.shape[0] : small].reshape(-1).astype(jnp.float32)
    first_gain = gains[:D]
    second_gain = gains[D : 2 * D]
    mixer_gain = gains[2 * D :]
    groups = AHEADS // KVHEADS
    stream = tokens.astype(jnp.float32)
    first_scale = rms_scale(stream)
    normed = (stream * first_scale * first_gain).astype(jnp.bfloat16)
    expanded = project(normed, w_first)[0]
    gate_branch = expanded[:, :DINNER]
    conv_input = expanded[:, DINNER:PROJ_AT].astype(jnp.bfloat16)
    raw_step = expanded[:, STEP_AT:small_at]
    projected = expanded[None, :, PROJ_AT:STEP_AT]
    edge = passed_along(conv_input[rows - (KCONV - 1) :], "ctx", 1)
    extended = jnp.concatenate([edge, conv_input], 0).astype(jnp.float32)
    mixed = conv_full[KCONV]
    for offset in range(KCONV):
        mixed = mixed + conv_full[offset] * extended[offset : offset + rows]
    mixed_sig = jax.nn.sigmoid(mixed)
    conv_act = mixed * mixed_sig
    inputs = conv_act[:, :DINNER]
    b_proj = conv_act[:, DINNER : DINNER + STATE]
    c_proj = conv_act[:, DINNER + STATE :]
    step_size = jax.nn.softplus(raw_step + head_rates[0])
    rate = jnp.exp(head_rates[1])
    log_decay = -step_size * rate
    lower = jnp.arange(rows)[:, None] >= jnp.arange(rows)[None, :]
    lower_ones = lower.astype(jnp.float32)
    cumul = jnp.dot(lower_ones, log_decay, precision=HIGH)
    cumul_t = cumul.T
    total = cumul[-1]
    decays = jnp.exp(jnp.where(lower[None], cumul_t[:, :, None] - cumul_t[:, None, :], -jnp.inf))
    intersection = times(c_proj, b_proj, ((1,), (1,)))
    mixing = (intersection[None] * decays).astype(jnp.bfloat16)
    stepped = inputs * spread(step_size)
    stepped_low = stepped.astype(jnp.bfloat16)
    stepped_heads = per_head(stepped_low)
    within = flat_heads(headed(mixing, stepped_heads))
    tail = spread(jnp.exp(total[None] - cumul))
    local_state = times(stepped * tail, b_proj, ((0,), (0,)))
    all_states = lax.all_gather(pack_state(local_state, total), "ctx", axis=0)
    totals = totals_of(all_states)
    turn = jnp.arange(ctx_count)
    reach_before = (turn[None, :] < here) & (turn[None, :] > turn[:, None])
    before = jnp.exp(jnp.einsum("kj,jh->kh", reach_before.astype(jnp.float32), totals, precision=HIGH))
    before = jnp.where((turn < here)[:, None], before, 0.0)
    reach_after = (turn[None, :] > here) & (turn[None, :] < turn[:, None])
    after = jnp.exp(jnp.einsum("kj,jh->kh", reach_after.astype(jnp.float32), totals, precision=HIGH))
    after = jnp.where((turn > here)[:, None], after, 0.0)
    entering = jnp.sum(spread(before)[:, :, None] * all_states[:, :DINNER].astype(jnp.float32), 0)
    grown = spread(jnp.exp(cumul))
    scan_out = within + grown * times(c_proj, entering, ((1,), (1,)))
    skip = spread(head_rates[2][None])
    scanned = scan_out + skip * inputs
    gate_sig = jax.nn.sigmoid(gate_branch)
    gate_act = gate_branch * gate_sig
    gated = (scanned * gate_act)[None]
    gated_scale = rms_scale(gated)
    gated_norm = (gated * gated_scale * mixer_gain).astype(jnp.bfloat16)
    mixer_branch = project(gated_norm, w_contract)
    query_pos = here * rows + jnp.arange(rows)
    positions = query_pos.astype(jnp.float32)
    queries = rotate(
        projected[..., : AHEADS * ADIM].reshape(batch, rows, AHEADS, ADIM), positions
    ).astype(jnp.bfloat16)
    keys = rotate(
        projected[..., AHEADS * ADIM : (AHEADS + KVHEADS) * ADIM].reshape(
            batch, rows, KVHEADS, ADIM
        ),
        positions,
    ).astype(jnp.bfloat16)
    values = (
        projected[..., (AHEADS + KVHEADS) * ADIM :]
        .reshape(batch, rows, KVHEADS, ADIM)
        .astype(jnp.bfloat16)
    )
    both = jnp.concatenate(
        [keys.reshape(batch, rows, -1), values.reshape(batch, rows, -1)], -1
    )
    both_all = lax.all_gather(both, "ctx", axis=1, tiled=True)
    key_all = both_all[..., : KVHEADS * ADIM].reshape(batch, -1, KVHEADS, ADIM)
    value_all = both_all[..., KVHEADS * ADIM :].reshape(batch, -1, KVHEADS, ADIM)
    key_pos = jnp.arange(rows * ctx_count)
    causal = key_pos[None, :] <= query_pos[:, None]
    grouped = queries.reshape(batch, rows, KVHEADS, groups, ADIM)
    scores = masked_scores(grouped, key_all, causal)
    maxima = jnp.max(scores, -1, keepdims=True)
    expos = jnp.exp(scores - maxima)
    totals = jnp.sum(expos, -1, keepdims=True)
    log_total = maxima + jnp.log(totals)
    probs = (expos / totals).astype(jnp.bfloat16)
    attended = jnp.einsum("bkgts,bskd->btkgd", probs, value_all, preferred_element_type=jnp.float32)
    attended = attended.reshape(batch, rows, AHEADS * ADIM).astype(jnp.bfloat16)
    attention_branch = project(attended, w_combine)
    middle = stream + mixer_branch + attention_branch
    second_scale = rms_scale(middle)
    second = (middle * second_scale * second_gain).astype(jnp.bfloat16)
    widened = project(second, w_widen)
    gate_value = widened[..., :FF]
    up_value = widened[..., FF:]
    feed_sig = jax.nn.sigmoid(gate_value)
    activated = (gate_value * feed_sig * up_value).astype(jnp.bfloat16)
    layer_output = (middle + project(activated, w_narrow)).astype(jnp.bfloat16)
    outer_grad = cotangent.astype(jnp.float32)
    narrow_grad = outer_sum(activated, cotangent)
    act_grad = project_back(cotangent, w_narrow)
    gate_grad = act_grad * up_value * feed_sig * (1.0 + gate_value * (1.0 - feed_sig))
    up_grad = act_grad * gate_value * feed_sig
    widened_grad = jnp.concatenate([gate_grad, up_grad], -1).astype(jnp.bfloat16)
    widen_grad = outer_sum(second, widened_grad)
    widen_own = scattered(widen_grad.astype(jnp.bfloat16))
    second_grad = project_back(widened_grad, w_widen)
    middle_part, second_gain_grad = rms_back(middle, second_scale, second_gain, second_grad)
    middle_grad = outer_grad + middle_part
    branch_grad = middle_grad.astype(jnp.bfloat16)
    combine_grad = outer_sum(attended, branch_grad)
    attended_grad = project_back(branch_grad, w_combine).astype(jnp.bfloat16)
    attended_grad = attended_grad.reshape(batch, rows, KVHEADS, groups, ADIM)
    scores = masked_scores(grouped, key_all, causal)
    float_probs = jnp.exp(scores - log_total)
    value_part = jnp.einsum(
        "bkgts,btkgd->bskd",
        float_probs.astype(jnp.bfloat16),
        attended_grad,
        preferred_element_type=jnp.float32,
    )
    probs_grad = jnp.einsum(
        "btkgd,bskd->bkgts", attended_grad, value_all, preferred_element_type=jnp.float32
    )
    centre = jnp.sum(probs_grad * float_probs, -1, keepdims=True)
    scores_grad = (float_probs * (probs_grad - centre)).astype(jnp.bfloat16)
    query_grad = ADIM ** (-0.5) * jnp.einsum(
        "bkgts,bskd->btkgd", scores_grad, key_all, preferred_element_type=jnp.float32
    )
    key_part = ADIM ** (-0.5) * jnp.einsum(
        "bkgts,btkgd->bskd", scores_grad, grouped, preferred_element_type=jnp.float32
    )
    keys_span = rows * ctx_count
    parts = jnp.concatenate(
        [
            key_part.astype(jnp.bfloat16).reshape(keys_span, -1),
            value_part.astype(jnp.bfloat16).reshape(keys_span, -1),
        ],
        -1,
    )
    part_sum = lax.psum_scatter(parts, "ctx", scatter_dimension=0, tiled=True).astype(jnp.float32)
    key_sum = part_sum[:, : KVHEADS * ADIM].reshape(batch, rows, KVHEADS, ADIM)
    value_sum = part_sum[:, KVHEADS * ADIM :].reshape(batch, rows, KVHEADS, ADIM)
    query_grad = rotate(query_grad.reshape(batch, rows, AHEADS, ADIM), -positions)
    key_sum = rotate(key_sum, -positions)
    projected_grad = jnp.concatenate(
        [
            query_grad.reshape(batch, rows, AHEADS * ADIM),
            key_sum.reshape(batch, rows, KVHEADS * ADIM),
            value_sum.reshape(batch, rows, KVHEADS * ADIM),
        ],
        -1,
    ).astype(jnp.bfloat16)
    contract_grad = outer_sum(gated_norm, branch_grad)
    second_sum = jnp.concatenate(
        [
            contract_grad.astype(jnp.bfloat16).reshape(devices, contract_rows, D),
            combine_grad.astype(jnp.bfloat16).reshape(devices, combine_rows, D),
            narrow_grad.astype(jnp.bfloat16).reshape(devices, narrow_rows, D),
        ],
        1,
    )
    second_own = scattered(second_sum)[0].astype(jnp.float32)
    gated_norm_grad = project_back(branch_grad, w_contract)
    gated_grad, mixer_gain_grad = rms_back(gated, gated_scale, mixer_gain, gated_norm_grad)
    gated_grad = gated_grad[0]
    scanned_grad = gated_grad * gate_act
    gate_branch_grad = gated_grad * scanned * gate_sig * (1.0 + gate_branch * (1.0 - gate_sig))
    outgoing = times(grown * scanned_grad, c_proj, ((0,), (0,)))
    all_grads = lax.all_gather(outgoing.astype(jnp.bfloat16), "ctx", axis=0)
    leaving = jnp.sum(spread(after)[:, :, None] * all_grads.astype(jnp.float32), 0)
    scanned_low = scanned_grad.astype(jnp.bfloat16)
    scanned_heads = per_head(scanned_low)
    mixing_grad = lax.dot_general(
        scanned_heads,
        stepped_heads,
        (((2,), (2,)), ((0,), (0,))),
        preferred_element_type=jnp.float32,
    )
    crossing = jnp.sum(mixing_grad * decays, 0)
    from_leaving = tail * times(b_proj, leaving, ((1,), (1,)))
    within_back = flat_heads(headed_t(mixing, scanned_heads))
    stepped_grad = within_back + from_leaving
    c_grad = times(crossing, b_proj, ((1,), (0,))) + times(
        grown * scanned_grad, entering, ((1,), (0,))
    )
    b_grad = times(crossing, c_proj, ((0,), (0,))) + times(tail * stepped, leaving, ((1,), (0,)))
    rounded_grad = scanned_low.astype(jnp.float32)
    rounded_step = stepped_low.astype(jnp.float32)
    tail_part = head_sum(stepped * from_leaving)
    cumul_grad = (
        head_sum(rounded_grad * within + scanned_grad * (scan_out - within))
        - head_sum(rounded_step * within_back)
        - tail_part
    )
    total_grad = jnp.sum(tail_part, 0) + jnp.exp(total) * jnp.sum(
        (leaving * entering).reshape(MHEADS, -1), -1
    )
    log_grad = (
        lax.dot_general(lower_ones, cumul_grad, (((0,), (0,)), ((), ())), precision=HIGH)
        + total_grad[None]
    )
    step_grad = head_sum(stepped_grad * inputs) - log_grad * rate
    raw_grad = step_grad * jax.nn.sigmoid(raw_step + head_rates[0])
    rates_local = jnp.stack(
        [
            jnp.sum(raw_grad, 0),
            jnp.sum(log_grad * log_decay, 0),
            jnp.sum(head_sum(scanned_grad * inputs), 0),
        ],
        0,
    )
    inputs_grad = stepped_grad * spread(step_size) + skip * scanned_grad
    act_back = jnp.concatenate([inputs_grad, b_grad, c_grad], 1)
    mixed_grad = act_back * mixed_sig * (1.0 + mixed * (1.0 - mixed_sig))
    conv_grad = jnp.stack(
        [jnp.sum(mixed_grad * extended[k : k + rows], 0) for k in range(KCONV)]
        + [jnp.sum(mixed_grad, 0)],
        0,
    )
    spill = jnp.concatenate([jnp.zeros((KCONV - 1, CONV_CH), jnp.float32), mixed_grad[: KCONV - 1]], 0)
    lead = sum(conv_full[k] * spill[KCONV - 1 - k : 2 * (KCONV - 1) - k] for k in range(KCONV - 1))
    returned = passed_along(lead, "ctx", -1)
    padded = jnp.concatenate([mixed_grad, jnp.zeros((KCONV - 1, CONV_CH), jnp.float32)], 0)
    conv_input_grad = sum(
        conv_full[k] * padded[KCONV - 1 - k : KCONV - 1 - k + rows] for k in range(KCONV)
    )
    conv_input_grad = conv_input_grad + jnp.concatenate(
        [jnp.zeros((rows - (KCONV - 1), CONV_CH), jnp.float32), returned], 0
    )
    rates_total = lax.psum(rates_local, ALL)
    first_back = jnp.concatenate(
        [
            gate_branch_grad.astype(jnp.bfloat16),
            conv_input_grad.astype(jnp.bfloat16),
            projected_grad[0],
            raw_grad.astype(jnp.bfloat16),
            jnp.zeros((rows, WIDE - small_at), jnp.bfloat16),
        ],
        1,
    )[None]
    normed_grad = project_back(first_back, w_first)
    input_part, first_gain_grad = rms_back(stream, first_scale, first_gain, normed_grad)
    input_gradient = middle_grad + input_part
    gains_local = jnp.concatenate([first_gain_grad, second_gain_grad, mixer_gain_grad], 0)
    small_grads = jnp.concatenate(
        [conv_grad.reshape(devices, -1), gains_local.reshape(devices, -1)], 1
    )
    small_grads = jnp.pad(small_grads, ((0, 0), (0, small_cols * count - small))).reshape(
        D, small_cols
    )
    first_grad = outer_sum(normed, first_back)
    first_sum = jnp.concatenate(
        [
            first_grad[:, :STEP_AT],
            jnp.concatenate(
                [
                    first_grad[:, STEP_AT:small_at],
                    small_grads,
                    jnp.zeros((D, WIDE - small_at - small_cols), jnp.float32),
                ],
                1,
            ),
        ],
        1,
    ).astype(jnp.bfloat16)
    first_own = scattered(first_sum).astype(jnp.float32)
    small_own = first_own[:, small_at : small_at + small_cols].reshape(-1)
    return (
        layer_output,
        input_gradient,
        jnp.concatenate([first_own[:, :PROJ_AT], first_own[:, STEP_AT:small_at]], 1).reshape(-1),
        small_own[: convolver.shape[0]],
        second_own[:contract_rows].reshape(-1),
        first_own[:, PROJ_AT:STEP_AT].reshape(-1),
        second_own[contract_rows : contract_rows + combine_rows].reshape(-1),
        widen_own.astype(jnp.float32).reshape(-1),
        second_own[contract_rows + combine_rows :].reshape(-1),
        small_own[convolver.shape[0] : small],
        rates_total,
    )


def solution(mesh):
    return jax.shard_map(
        local,
        mesh=mesh,
        in_specs=(
            P("dp", "ctx", None),
            P("dp", "ctx", None),
            P(("dp", "ctx")),
            P(("dp", "ctx")),
            P(("dp", "ctx")),
            P(("dp", "ctx")),
            P(("dp", "ctx")),
            P(("dp", "ctx")),
            P(("dp", "ctx")),
            P(("dp", "ctx")),
            P(),
        ),
        out_specs=(
            P("dp", "ctx", None),
            P("dp", "ctx", None),
            P(("dp", "ctx")),
            P(("dp", "ctx")),
            P(("dp", "ctx")),
            P(("dp", "ctx")),
            P(("dp", "ctx")),
            P(("dp", "ctx")),
            P(("dp", "ctx")),
            P(("dp", "ctx")),
            P(),
        ),
        check_vma=False,
    )
```

```python
import jax
import jax.numpy as jnp
from jax import lax
from jax.sharding import PartitionSpec as P

D = 1024
MHEADS = 24
MDIM = 64
STATE = 128
KCONV = 4
AHEADS = 8
KVHEADS = 2
ADIM = 64
FF = 2048
SPAN = 128
DINNER = 1536
CONV_CH = 1792
PROJ = 3352


EPSILON = 1e-05
ROPE_BASE = 10000.0


def passed_along(value, axis, steps):
    count = lax.axis_size(axis)
    leading, last = (max(0, -steps), min(count, count - steps))
    return lax.ppermute(value, axis, [(source, source + steps) for source in range(leading, last)])


def turned(value, steps):
    count = lax.axis_size("ctx")
    return lax.ppermute(value, "ctx", [(at, (at + steps) % count) for at in range(count)])


def around(value):
    return [value] + [turned(value, k) for k in range(1, lax.axis_size("ctx"))]


def rms_scale(values):
    return lax.rsqrt(jnp.mean(values * values, -1, keepdims=True) + EPSILON)


def rms_back(values, scale, gain, grad):
    scaled = grad * gain
    values_grad = scale * scaled - values * scale**3 * jnp.mean(scaled * values, -1, keepdims=True)
    gain_grad = jnp.sum(grad * values * scale, axis=(0, 1))
    return (values_grad, gain_grad)


def rotate(values, positions):
    half = values.shape[-1] // 2
    freqs = ROPE_BASE ** (-(jnp.arange(half).astype(jnp.float32) * 2.0 / values.shape[-1]))
    angles = positions[:, None] * freqs[None, :]
    cosine = jnp.cos(angles)[:, None, :]
    sine = jnp.sin(angles)[:, None, :]
    first = values[..., :half]
    second = values[..., half:]
    return jnp.concatenate([first * cosine - second * sine, second * cosine + first * sine], -1)


def masked_scores(grouped, key_all, causal):
    raw_scores = jnp.einsum(
        "btkgd,bskd->bkgts", grouped, key_all, preferred_element_type=jnp.float32
    ) * ADIM ** (-0.5)
    return jnp.where(causal, raw_scores, -jnp.inf)


def project(left, right):
    return jnp.einsum("btd,df->btf", left, right, preferred_element_type=jnp.float32)


def project_back(left, right):
    return jnp.einsum("btf,df->btd", left, right, preferred_element_type=jnp.float32)


def outer_sum(left, right):
    return jnp.einsum("btd,btf->df", left, right, preferred_element_type=jnp.float32)


WIDE = 4224
STEP_AT = DINNER + CONV_CH + (AHEADS + 2 * KVHEADS) * ADIM
PROJ_AT = DINNER + CONV_CH
ALL = ("dp", "ctx")
HIGH = lax.Precision.HIGHEST


def gathered(shard):
    return lax.all_gather(shard, ALL, axis=0, tiled=True)


def scattered(value):
    return lax.psum_scatter(value, ALL, scatter_dimension=0, tiled=True)


def per_head(values):
    return jnp.transpose(values.reshape(values.shape[0], MHEADS, MDIM), (1, 0, 2))


def flat_heads(values):
    return jnp.transpose(values, (1, 0, 2)).reshape(values.shape[1], DINNER)


def spread(per_step):
    return jnp.repeat(per_step, MDIM, axis=1)


def headed(left, right):
    return lax.dot_general(
        left.astype(jnp.bfloat16),
        right.astype(jnp.bfloat16),
        (((2,), (1,)), ((0,), (0,))),
        preferred_element_type=jnp.float32,
    )


def headed_t(left, right):
    return lax.dot_general(
        left.astype(jnp.bfloat16),
        right.astype(jnp.bfloat16),
        (((1,), (1,)), ((0,), (0,))),
        preferred_element_type=jnp.float32,
    )


def times(left, right, dims):
    return lax.dot_general(
        left.astype(jnp.bfloat16),
        right.astype(jnp.bfloat16),
        (dims, ((), ())),
        preferred_element_type=jnp.float32,
    )


def pack_state(state, total):
    lead = total.astype(jnp.bfloat16)
    rest = (total - lead.astype(jnp.float32)).astype(jnp.bfloat16)
    extra = jnp.zeros((16, STATE), jnp.bfloat16)
    extra = extra.at[0, :MHEADS].set(lead).at[1, :MHEADS].set(rest)
    return jnp.concatenate([state.astype(jnp.bfloat16), extra], 0)


def totals_of(packed):
    parts = packed[:, DINNER : DINNER + 2, :MHEADS].astype(jnp.float32)
    return parts[:, 0] + parts[:, 1]


def head_sum(values):
    return jnp.sum(values.reshape(values.shape[0], MHEADS, MDIM), -1)


def local(
    tokens,
    cotangent,
    expander,
    convolver,
    contractor,
    projector,
    combiner,
    widener,
    narrower,
    norm_gains,
    head_rates,
):
    devices = lax.axis_size("dp") * lax.axis_size("ctx")
    ctx_count = lax.axis_size("ctx")
    here = lax.axis_index("ctx")
    batch, rows = (tokens.shape[0], tokens.shape[1])
    count = D // devices
    small = convolver.shape[0] + norm_gains.shape[0]
    small_cols = -(-small // count)
    small_at = STEP_AT + MHEADS
    small_all = jnp.pad(
        jnp.concatenate([convolver, norm_gains], 0), (0, small_cols * count - small)
    ).reshape(count, small_cols)
    expander_rows = expander.reshape(count, PROJ)
    shard_first = jnp.concatenate(
        [
            expander_rows[:, :PROJ_AT],
            projector.reshape(count, -1),
            expander_rows[:, PROJ_AT:],
            small_all,
            jnp.zeros((count, WIDE - small_at - small_cols), jnp.bfloat16),
        ],
        1,
    )
    w_first = gathered(shard_first)
    contract_rows, combine_rows, narrow_rows = (
        DINNER // devices,
        AHEADS * ADIM // devices,
        FF // devices,
    )
    shard_second = jnp.concatenate(
        [
            contractor.reshape(contract_rows, D),
            combiner.reshape(combine_rows, D),
            narrower.reshape(narrow_rows, D),
        ],
        0,
    )
    shard_second, w_first = lax.optimization_barrier((shard_second, w_first))
    w_second = gathered(shard_second[None])
    w_contract = w_second[:, :contract_rows].reshape(DINNER, D)
    w_combine = w_second[:, contract_rows : contract_rows + combine_rows].reshape(AHEADS * ADIM, D)
    w_narrow = w_second[:, contract_rows + combine_rows :].reshape(FF, D)
    shard_widen, w_second_done = lax.optimization_barrier((widener.reshape(count, 2 * FF), w_second[0, 0, 0]))
    w_widen = gathered(shard_widen)

    small_back = w_first[:, small_at : small_at + small_cols].reshape(devices, -1)
    conv_full = small_back[:, : convolver.shape[0]].reshape(KCONV + 1, CONV_CH).astype(jnp.float32)
    gains = small_back[:, convolver.shape[0] : small].reshape(-1).astype(jnp.float32)
    first_gain = gains[:D]
    second_gain = gains[D : 2 * D]
    mixer_gain = gains[2 * D :]
    groups = AHEADS // KVHEADS
    stream = tokens.astype(jnp.float32)
    first_scale = rms_scale(stream)
    normed = (stream * first_scale * first_gain).astype(jnp.bfloat16)
    expanded = project(normed, w_first)[0]
    gate_branch = expanded[:, :DINNER]
    conv_input = expanded[:, DINNER:PROJ_AT].astype(jnp.bfloat16)
    raw_step = expanded[:, STEP_AT:small_at]
    projected = expanded[None, :, PROJ_AT:STEP_AT]
    edge = passed_along(conv_input[rows - (KCONV - 1) :], "ctx", 1)
    extended = jnp.concatenate([edge, conv_input], 0).astype(jnp.float32)
    mixed = conv_full[KCONV]
    for offset in range(KCONV):
        mixed = mixed + conv_full[offset] * extended[offset : offset + rows]
    mixed_sig = jax.nn.sigmoid(mixed)
    conv_act = mixed * mixed_sig
    inputs = conv_act[:, :DINNER]
    b_proj = conv_act[:, DINNER : DINNER + STATE]
    c_proj = conv_act[:, DINNER + STATE :]
    step_size = jax.nn.softplus(raw_step + head_rates[0])
    rate = jnp.exp(head_rates[1])
    log_decay = -step_size * rate
    lower = jnp.arange(rows)[:, None] >= jnp.arange(rows)[None, :]
    lower_ones = lower.astype(jnp.float32)
    cumul = jnp.dot(lower_ones, log_decay, precision=HIGH)
    cumul_t = cumul.T
    total = cumul[-1]
    decays = jnp.exp(jnp.where(lower[None], cumul_t[:, :, None] - cumul_t[:, None, :], -jnp.inf))
    intersection = times(c_proj, b_proj, ((1,), (1,)))
    mixing = (intersection[None] * decays).astype(jnp.bfloat16)
    stepped = inputs * spread(step_size)
    stepped_low = stepped.astype(jnp.bfloat16)
    stepped_heads = per_head(stepped_low)
    within = flat_heads(headed(mixing, stepped_heads))
    tail = spread(jnp.exp(total[None] - cumul))
    local_state = times(stepped * tail, b_proj, ((0,), (0,)))
    all_states = jnp.stack(around(pack_state(local_state, total)), 0)
    totals = totals_of(all_states)
    turn = (here + ctx_count - jnp.arange(ctx_count)) % ctx_count
    reach_before = (turn[None, :] < here) & (turn[None, :] > turn[:, None])
    before = jnp.exp(jnp.einsum("kj,jh->kh", reach_before.astype(jnp.float32), totals, precision=HIGH))
    before = jnp.where((turn < here)[:, None], before, 0.0)
    reach_after = (turn[None, :] > here) & (turn[None, :] < turn[:, None])
    after = jnp.exp(jnp.einsum("kj,jh->kh", reach_after.astype(jnp.float32), totals, precision=HIGH))
    after = jnp.where((turn > here)[:, None], after, 0.0)
    entering = jnp.sum(spread(before)[:, :, None] * all_states[:, :DINNER].astype(jnp.float32), 0)
    grown = spread(jnp.exp(cumul))
    scan_out = within + grown * times(c_proj, entering, ((1,), (1,)))
    skip = spread(head_rates[2][None])
    scanned = scan_out + skip * inputs
    gate_sig = jax.nn.sigmoid(gate_branch)
    gate_act = gate_branch * gate_sig
    gated = (scanned * gate_act)[None]
    gated_scale = rms_scale(gated)
    gated_norm = (gated * gated_scale * mixer_gain).astype(jnp.bfloat16)
    mixer_branch = project(gated_norm, w_contract)
    query_pos = here * rows + jnp.arange(rows)
    positions = query_pos.astype(jnp.float32)
    queries = rotate(
        projected[..., : AHEADS * ADIM].reshape(batch, rows, AHEADS, ADIM), positions
    ).astype(jnp.bfloat16)
    keys = rotate(
        projected[..., AHEADS * ADIM : (AHEADS + KVHEADS) * ADIM].reshape(
            batch, rows, KVHEADS, ADIM
        ),
        positions,
    ).astype(jnp.bfloat16)
    values = (
        projected[..., (AHEADS + KVHEADS) * ADIM :]
        .reshape(batch, rows, KVHEADS, ADIM)
        .astype(jnp.bfloat16)
    )
    both = jnp.concatenate(
        [keys.reshape(batch, rows, -1), values.reshape(batch, rows, -1)], -1
    )
    both_all = jnp.concatenate(around(both), 1)
    key_all = both_all[..., : KVHEADS * ADIM].reshape(batch, -1, KVHEADS, ADIM)
    value_all = both_all[..., KVHEADS * ADIM :].reshape(batch, -1, KVHEADS, ADIM)
    sources = (here + ctx_count - jnp.arange(ctx_count)) % ctx_count
    key_pos = (sources[:, None] * rows + jnp.arange(rows)[None, :]).reshape(-1)
    causal = key_pos[None, :] <= query_pos[:, None]
    grouped = queries.reshape(batch, rows, KVHEADS, groups, ADIM)
    scores = masked_scores(grouped, key_all, causal)
    maxima = jnp.max(scores, -1, keepdims=True)
    expos = jnp.exp(scores - maxima)
    totals = jnp.sum(expos, -1, keepdims=True)
    log_total = maxima + jnp.log(totals)
    probs = (expos / totals).astype(jnp.bfloat16)
    attended = jnp.einsum("bkgts,bskd->btkgd", probs, value_all, preferred_element_type=jnp.float32)
    attended = attended.reshape(batch, rows, AHEADS * ADIM).astype(jnp.bfloat16)
    attention_branch = project(attended, w_combine)
    middle = stream + mixer_branch + attention_branch
    second_scale = rms_scale(middle)
    second = (middle * second_scale * second_gain).astype(jnp.bfloat16)
    widened = project(second, w_widen)
    gate_value = widened[..., :FF]
    up_value = widened[..., FF:]
    feed_sig = jax.nn.sigmoid(gate_value)
    activated = (gate_value * feed_sig * up_value).astype(jnp.bfloat16)
    layer_output = (middle + project(activated, w_narrow)).astype(jnp.bfloat16)
    outer_grad = cotangent.astype(jnp.float32)
    narrow_grad = outer_sum(activated, cotangent)
    act_grad = project_back(cotangent, w_narrow)
    gate_grad = act_grad * up_value * feed_sig * (1.0 + gate_value * (1.0 - feed_sig))
    up_grad = act_grad * gate_value * feed_sig
    widened_grad = jnp.concatenate([gate_grad, up_grad], -1).astype(jnp.bfloat16)
    widen_grad = outer_sum(second, widened_grad)
    widen_sum, widened_grad = lax.optimization_barrier(
        (widen_grad.astype(jnp.bfloat16), widened_grad)
    )
    widen_own = scattered(widen_sum)
    second_grad = project_back(widened_grad, w_widen)
    middle_part, second_gain_grad = rms_back(middle, second_scale, second_gain, second_grad)
    middle_grad = outer_grad + middle_part
    branch_grad = middle_grad.astype(jnp.bfloat16)
    combine_grad = outer_sum(attended, branch_grad)
    attended_grad = project_back(branch_grad, w_combine).astype(jnp.bfloat16)
    attended_grad = attended_grad.reshape(batch, rows, KVHEADS, groups, ADIM)
    scores = masked_scores(grouped, key_all, causal)
    float_probs = jnp.exp(scores - log_total)
    value_part = jnp.einsum(
        "bkgts,btkgd->bskd",
        float_probs.astype(jnp.bfloat16),
        attended_grad,
        preferred_element_type=jnp.float32,
    )
    probs_grad = jnp.einsum(
        "btkgd,bskd->bkgts", attended_grad, value_all, preferred_element_type=jnp.float32
    )
    centre = jnp.sum(probs_grad * float_probs, -1, keepdims=True)
    scores_grad = (float_probs * (probs_grad - centre)).astype(jnp.bfloat16)
    query_grad = ADIM ** (-0.5) * jnp.einsum(
        "bkgts,bskd->btkgd", scores_grad, key_all, preferred_element_type=jnp.float32
    )
    key_part = ADIM ** (-0.5) * jnp.einsum(
        "bkgts,btkgd->bskd", scores_grad, grouped, preferred_element_type=jnp.float32
    )
    keys_span = rows * ctx_count
    parts = jnp.concatenate(
        [
            key_part.astype(jnp.bfloat16).reshape(keys_span, -1),
            value_part.astype(jnp.bfloat16).reshape(keys_span, -1),
        ],
        -1,
    )
    part_sum = parts[:rows].astype(jnp.float32)
    for k in range(1, ctx_count):
        part_sum = part_sum + turned(parts[k * rows : (k + 1) * rows], -k).astype(jnp.float32)
    key_sum = part_sum[:, : KVHEADS * ADIM].reshape(batch, rows, KVHEADS, ADIM)
    value_sum = part_sum[:, KVHEADS * ADIM :].reshape(batch, rows, KVHEADS, ADIM)
    query_grad = rotate(query_grad.reshape(batch, rows, AHEADS, ADIM), -positions)
    key_sum = rotate(key_sum, -positions)
    projected_grad = jnp.concatenate(
        [
            query_grad.reshape(batch, rows, AHEADS * ADIM),
            key_sum.reshape(batch, rows, KVHEADS * ADIM),
            value_sum.reshape(batch, rows, KVHEADS * ADIM),
        ],
        -1,
    ).astype(jnp.bfloat16)
    contract_grad = outer_sum(gated_norm, branch_grad)
    second_sum = jnp.concatenate(
        [
            contract_grad.astype(jnp.bfloat16).reshape(devices, contract_rows, D),
            combine_grad.astype(jnp.bfloat16).reshape(devices, combine_rows, D),
            narrow_grad.astype(jnp.bfloat16).reshape(devices, narrow_rows, D),
        ],
        1,
    )
    second_sum, branch_grad = lax.optimization_barrier((second_sum, branch_grad))
    second_sum, widen_own = lax.optimization_barrier((second_sum, widen_own))
    second_own = scattered(second_sum)[0]
    gated_norm_grad = project_back(branch_grad, w_contract)
    gated_grad, mixer_gain_grad = rms_back(gated, gated_scale, mixer_gain, gated_norm_grad)
    gated_grad = gated_grad[0]
    scanned_grad = gated_grad * gate_act
    gate_branch_grad = gated_grad * scanned * gate_sig * (1.0 + gate_branch * (1.0 - gate_sig))
    outgoing = times(grown * scanned_grad, c_proj, ((0,), (0,)))
    all_grads = jnp.stack(around(outgoing.astype(jnp.bfloat16)), 0)
    leaving = jnp.sum(spread(after)[:, :, None] * all_grads.astype(jnp.float32), 0)
    scanned_low = scanned_grad.astype(jnp.bfloat16)
    scanned_heads = per_head(scanned_low)
    mixing_grad = lax.dot_general(
        scanned_heads,
        stepped_heads,
        (((2,), (2,)), ((0,), (0,))),
        preferred_element_type=jnp.float32,
    )
    crossing = jnp.sum(mixing_grad * decays, 0)
    from_leaving = tail * times(b_proj, leaving, ((1,), (1,)))
    within_back = flat_heads(headed_t(mixing, scanned_heads))
    stepped_grad = within_back + from_leaving
    c_grad = times(crossing, b_proj, ((1,), (0,))) + times(
        grown * scanned_grad, entering, ((1,), (0,))
    )
    b_grad = times(crossing, c_proj, ((0,), (0,))) + times(tail * stepped, leaving, ((1,), (0,)))
    rounded_grad = scanned_low.astype(jnp.float32)
    rounded_step = stepped_low.astype(jnp.float32)
    tail_part = head_sum(stepped * from_leaving)
    cumul_grad = (
        head_sum(rounded_grad * within + scanned_grad * (scan_out - within))
        - head_sum(rounded_step * within_back)
        - tail_part
    )
    total_grad = jnp.sum(tail_part, 0) + jnp.exp(total) * jnp.sum(
        (leaving * entering).reshape(MHEADS, -1), -1
    )
    log_grad = (
        lax.dot_general(lower_ones, cumul_grad, (((0,), (0,)), ((), ())), precision=HIGH)
        + total_grad[None]
    )
    step_grad = head_sum(stepped_grad * inputs) - log_grad * rate
    raw_grad = step_grad * jax.nn.sigmoid(raw_step + head_rates[0])
    rates_local = jnp.stack(
        [
            jnp.sum(raw_grad, 0),
            jnp.sum(log_grad * log_decay, 0),
            jnp.sum(head_sum(scanned_grad * inputs), 0),
        ],
        0,
    )
    inputs_grad = stepped_grad * spread(step_size) + skip * scanned_grad
    act_back = jnp.concatenate([inputs_grad, b_grad, c_grad], 1)
    mixed_grad = act_back * mixed_sig * (1.0 + mixed * (1.0 - mixed_sig))
    conv_grad = jnp.stack(
        [jnp.sum(mixed_grad * extended[k : k + rows], 0) for k in range(KCONV)]
        + [jnp.sum(mixed_grad, 0)],
        0,
    )
    spill = jnp.concatenate([jnp.zeros((KCONV - 1, CONV_CH), jnp.float32), mixed_grad[: KCONV - 1]], 0)
    lead = sum(conv_full[k] * spill[KCONV - 1 - k : 2 * (KCONV - 1) - k] for k in range(KCONV - 1))
    returned = passed_along(lead, "ctx", -1)
    padded = jnp.concatenate([mixed_grad, jnp.zeros((KCONV - 1, CONV_CH), jnp.float32)], 0)
    conv_input_grad = sum(
        conv_full[k] * padded[KCONV - 1 - k : KCONV - 1 - k + rows] for k in range(KCONV)
    )
    conv_input_grad = conv_input_grad + jnp.concatenate(
        [jnp.zeros((rows - (KCONV - 1), CONV_CH), jnp.float32), returned], 0
    )
    first_back = jnp.concatenate(
        [
            gate_branch_grad.astype(jnp.bfloat16),
            conv_input_grad.astype(jnp.bfloat16),
            projected_grad[0],
            raw_grad.astype(jnp.bfloat16),
            jnp.zeros((rows, WIDE - small_at), jnp.bfloat16),
        ],
        1,
    )[None]
    normed_grad = project_back(first_back, w_first)
    input_part, first_gain_grad = rms_back(stream, first_scale, first_gain, normed_grad)
    input_gradient = middle_grad + input_part
    gains_local = jnp.concatenate([first_gain_grad, second_gain_grad, mixer_gain_grad], 0)
    small_grads = jnp.concatenate(
        [conv_grad.reshape(devices, -1), gains_local.reshape(devices, -1)], 1
    )
    small_grads = jnp.pad(small_grads, ((0, 0), (0, small_cols * count - small))).reshape(
        D, small_cols
    )
    first_grad = outer_sum(normed, first_back)
    first_low = first_grad.astype(jnp.bfloat16)
    last_columns = jnp.concatenate(
        [
            first_low[:, STEP_AT:small_at],
            small_grads.astype(jnp.bfloat16),
            jnp.zeros((D, WIDE - small_at - small_cols), jnp.bfloat16),
        ],
        1,
    )
    first_sum = lax.dynamic_update_slice(first_low, last_columns, (0, STEP_AT))
    first_sum, rates_local, second_own = lax.optimization_barrier(
        (first_sum, rates_local, second_own)
    )
    second_own = second_own.astype(jnp.float32)
    rates_total = lax.psum(rates_local, ALL)
    first_own = scattered(first_sum).astype(jnp.float32)
    small_own = first_own[:, small_at : small_at + small_cols].reshape(-1)
    return (
        layer_output,
        input_gradient,
        jnp.concatenate([first_own[:, :PROJ_AT], first_own[:, STEP_AT:small_at]], 1).reshape(-1),
        small_own[: convolver.shape[0]],
        second_own[:contract_rows].reshape(-1),
        first_own[:, PROJ_AT:STEP_AT].reshape(-1),
        second_own[contract_rows : contract_rows + combine_rows].reshape(-1),
        widen_own.astype(jnp.float32).reshape(-1),
        second_own[contract_rows + combine_rows :].reshape(-1),
        small_own[convolver.shape[0] : small],
        rates_total,
    )


def solution(mesh):
    return jax.shard_map(
        local,
        mesh=mesh,
        in_specs=(
            P("dp", "ctx", None),
            P("dp", "ctx", None),
            P(("dp", "ctx")),
            P(("dp", "ctx")),
            P(("dp", "ctx")),
            P(("dp", "ctx")),
            P(("dp", "ctx")),
            P(("dp", "ctx")),
            P(("dp", "ctx")),
            P(("dp", "ctx")),
            P(),
        ),
        out_specs=(
            P("dp", "ctx", None),
            P("dp", "ctx", None),
            P(("dp", "ctx")),
            P(("dp", "ctx")),
            P(("dp", "ctx")),
            P(("dp", "ctx")),
            P(("dp", "ctx")),
            P(("dp", "ctx")),
            P(("dp", "ctx")),
            P(("dp", "ctx")),
            P(),
        ),
        check_vma=False,
    )
```
